32 devices in a mesh: segment: 4 (over z), dp: 8 (over y, x, core).
Axes of the slice: x: 2, y: 2, z: 4, core: 2. Of those that a mesh axis runs over, the one named last changes fastest.
Arguments:
- tokens: bfloat16 [4, 256, 6144], P(None, 'dp'), may hold values from -18 to 18
- norm_gain: bfloat16 [6144], replicated, may hold values from 0.099609375 to 1.8984375
- router_weight: bfloat16 [6144, 4], replicated, may hold values from -0.078125 to 0.078125
- expert_ids: int32 [4, 256, 2], P(None, 'dp'), may hold values from 0 to 3, all different within a row; in each aligned block of 32 rows (0 to 31, 32 to 63, ..., all dimensions but the last counted through in order) at most 20 rows name the same one
- w_gate: bfloat16 [4, 6144, 8192], P('segment', None, 'dp'), may hold values from -0.078125 to 0.078125
- w_up: bfloat16 [4, 6144, 8192], P('segment', None, 'dp'), may hold values from -0.078125 to 0.078125
- w_down: bfloat16 [4, 8192, 6144], P('segment', 'dp'), may hold values from -0.0625 to 0.0625
Outputs:
- scored: bfloat16 [4, 256, 6144], P(None, 'dp', 'segment')
The draws below stay inside these ranges and needn't reach their ends.
Inputs may be any that keep to these rules, and one draw needn't show every extreme that they name: `expert_ids`: each token names two different experts. In each micro-batch the 32 rows of one device name each expert at most 20 times, and in every draw some expert is named exactly 20 times by some device's rows.
All inputs are finite; a program needn't handle non-finite values.
Results may differ from the reference program's by a relative error of at most 0.0035.
Values may be sent and summed in bfloat16 or wider, within the bound.
No kernel may reach another device: no remote copies, remote signals or barrier semaphores. Data moves between devices by JAX's collectives and lax.ppermute only.
A program may use at most 128 MiB of HBM per device.

```python
import math
import jax
import jax.numpy as jnp
import numpy as np
from jax import lax

D = 6144
FF = 8192
MICRO = 4
TOK_DEV = 32
EXPERTS = 4
TOKENS = 256
CAP = 20
N_DP = 8


def draw_tokens(key, part):
    base_key, row_key = jax.random.split(key, 2)
    base = jnp.clip(jax.random.normal(base_key, (MICRO, TOKENS, D), jnp.float32), -6.0, 6.0)
    row_scale = jnp.exp(jax.random.uniform(row_key, (MICRO, TOKENS, 1), jnp.float32, math.log(0.3), math.log(3.0)))
    values = base * row_scale
    return values.astype(jnp.bfloat16)


def level_of(rng, extent, cuts, low, top_value):
    def one(dim, shards_of):
        draws = jax.random.uniform(jax.random.fold_in(jax.random.fold_in(rng, 6), dim), (shards_of,), jnp.float32, low / len(cuts), top_value / len(cuts))
        return jnp.repeat(jnp.exp(draws), extent[dim] // shards_of).reshape((-1,) + (1,) * (len(extent) - dim - 1))

    gain = one(*cuts[0])
    for cut in cuts[1:]:
        gain = gain * one(*cut)
    return gain


def shared_out(rng, own, number, rows, amount, top, reach, skew):
    order = jax.random.permutation(rng, amount)
    heavy_load, usual = load_shares(amount, rows * top, reach, skew, True), load_shares(amount, rows * top, reach, skew, False)
    places = jnp.arange(amount)

    def named(tallies, rotation):
        used = int((tallies > 0).sum())
        fixed = max(1, used // 4)
        moved = fixed + (places - fixed + rotation * (used - fixed)) % max(1, amount - fixed)
        return jnp.zeros((amount,), jnp.int32).at[order[jnp.where(places < fixed, places, moved)]].set(jnp.asarray(tallies, jnp.int32))

    tallies = jnp.where(number % 4 == 0, named(heavy_load, number // 4), named(usual, number - number // 4 - 1))
    mixed = jax.random.permutation(jax.random.fold_in(own, 3), amount)
    giver, receiver = mixed[0:amount // 2 * 2:2], mixed[1:amount // 2 * 2:2]
    slack = jnp.minimum(tallies[giver] - 1, reach - tallies[receiver]) // 2
    slack = jnp.where((giver == order[0]) | (receiver == order[0]) | (tallies[receiver] == 0), 0, jnp.maximum(slack, 0))
    moved = jax.random.randint(jax.random.fold_in(own, 4), (amount // 2,), 0, 1 << 20) % (slack + 1)
    tallies = tallies.at[giver].add(-moved).at[receiver].add(moved)
    items = jnp.searchsorted(jnp.cumsum(tallies), jnp.arange(rows * top), side="right").astype(jnp.int32)
    grid = items.reshape(top, rows).T
    grid = grid[jax.random.permutation(jax.random.fold_in(own, 1), rows)]
    rotation = jax.random.randint(jax.random.fold_in(own, 2), (rows, 1), 0, top)
    return jnp.take_along_axis(grid, (jnp.arange(top)[None, :] + rotation) % top, axis=1)


def load_shares(count, total, limit, slope, full):
    portions = [(1 << 20) // math.isqrt(standing ** slope) + 1 for standing in range(1, count + 1)]
    largest = limit if full else min(limit, max(-(-total // count), total * portions[0] // sum(portions)))
    least = 1 if total - largest >= count - 1 else 0
    given, surplus = [largest] + [least] * (count - 1), total - largest - least * (count - 1)
    while surplus > 0:
        free = [i for i in range(1, count) if given[i] < largest] or [i for i in range(1, count) if given[i] < limit]
        pool, left = sum([portions[i] for i in free]), surplus
        for i in free:
            addition = min(limit - given[i], max(1, left * portions[i] // pool), surplus)
            given[i] = given[i] + addition
            surplus = surplus - addition
    return np.array(given)


def gaussian(stream_key, shape, width, limit, pieces=(), held_as=jnp.bfloat16):
    level = level_of(stream_key, shape, pieces, -0.22, 0.18) if pieces else 1.0
    values = jax.random.normal(stream_key, shape, jnp.float32) * width * level
    return jnp.minimum(jnp.maximum(values, -limit), limit).astype(held_as)


def setup_inputs(seed: int = 0) -> dict:
    key_of = jax.random.split(jax.random.key(seed), 8)
    tokens = draw_tokens(jax.random.fold_in(key_of[7], 71), 0)
    norm_gain = jnp.clip(1.0 + 0.18 * jax.random.normal(key_of[1], (D,), jnp.float32), 0.099609375, 1.8984375).astype(jnp.bfloat16)
    router_weight = gaussian(key_of[2], (D, EXPERTS), D ** -0.5, 0.078125)
    expert_ids_keys = jax.random.split(jax.random.fold_in(key_of[3], 1), MICRO * TOKENS // TOK_DEV)
    expert_ids_turns = jax.random.permutation(jax.random.fold_in(key_of[3], 3), MICRO * TOKENS // TOK_DEV)
    expert_ids = jax.vmap(lambda own, number: shared_out(jax.random.fold_in(key_of[3], 2), own, number, TOK_DEV, EXPERTS, 2, CAP, 2))(expert_ids_keys, expert_ids_turns).reshape((MICRO, TOKENS, 2))
    w_gate = gaussian(key_of[4], (EXPERTS, D, FF), D ** -0.5, 0.078125, ((0, 4), (2, 8)))
    w_up = gaussian(key_of[5], (EXPERTS, D, FF), D ** -0.5, 0.078125, ((0, 4), (2, 8)))
    w_down = gaussian(key_of[6], (EXPERTS, FF, D), FF ** -0.5, 0.0625, ((0, 4), (1, 8)))
    return dict(tokens=tokens, norm_gain=norm_gain, router_weight=router_weight, expert_ids=expert_ids, w_gate=w_gate, w_up=w_up, w_down=w_down)


epsilon = 1e-05

def rms_normed(tokens, norm_gain):
    widened = tokens.astype(jnp.float32)
    inverse_rms = lax.rsqrt(lax.optimization_barrier(jnp.mean(widened * widened, axis=-1, keepdims=True)) + epsilon)
    return (widened, (widened * inverse_rms * norm_gain.astype(jnp.float32)).astype(jnp.bfloat16))

def pair_gates(pair_ids, logits):
    expert_range = jnp.arange(logits.shape[-1], dtype=jnp.int32)
    first_logit = lax.optimization_barrier(jnp.sum(jnp.where(pair_ids[..., 0:1] == expert_range, logits, 0.0), axis=-1))
    second_logit = lax.optimization_barrier(jnp.sum(jnp.where(pair_ids[..., 1:2] == expert_range, logits, 0.0), axis=-1))
    return (jax.nn.sigmoid(first_logit - second_logit), jax.nn.sigmoid(second_logit - first_logit))

def expert_weight(pair_ids, first_gate, second_gate, expert):
    return jnp.where(pair_ids[..., 0] == expert, first_gate, 0.0) + jnp.where(pair_ids[..., 1] == expert, second_gate, 0.0)

def slot_table(pair_ids, expert, slot_count):
    chosen = jnp.any(pair_ids == expert, axis=-1)
    hit_count = chosen.astype(jnp.int32)
    position = jnp.cumsum(hit_count, axis=-1) - hit_count
    slot_range = jnp.arange(slot_count, dtype=jnp.int32)
    dispatch = chosen[..., None, :] & (position[..., None, :] == slot_range[:, None])
    return (position, dispatch)

def reference(tokens, norm_gain, router_weight, expert_ids, w_gate, w_up, w_down):
    widened, normed = rms_normed(tokens, norm_gain)
    logits = jnp.dot(normed.reshape(-1, D), router_weight, preferred_element_type=jnp.float32)
    logits = logits.reshape(MICRO, TOKENS, EXPERTS)
    first_gate, second_gate = pair_gates(expert_ids, logits)
    block_ids = expert_ids.reshape(MICRO, N_DP, TOK_DEV, 2)
    block_rows = normed.reshape(MICRO, N_DP, TOK_DEV, D).astype(jnp.float32)
    unit_count = FF // N_DP

    def add_expert(summed, expert):
        position, dispatch = slot_table(block_ids, expert, CAP)
        dispatch_float = dispatch.astype(jnp.float32)
        routed = jnp.einsum('mgct,mgtf->mgcf', dispatch_float, block_rows).astype(jnp.bfloat16)
        row_block = routed.reshape(-1, D)
        gate_proj = jnp.dot(row_block, w_gate[expert], preferred_element_type=jnp.float32)
        up_proj = jnp.dot(row_block, w_up[expert], preferred_element_type=jnp.float32)
        hidden = (jax.nn.silu(gate_proj) * up_proj).astype(jnp.bfloat16)
        down_matrix = w_down[expert]

        def add_units(accumulated, shard):
            units = lax.dynamic_slice_in_dim(hidden, shard * unit_count, unit_count, 1)
            down_rows = lax.dynamic_slice_in_dim(down_matrix, shard * unit_count, unit_count, 0)
            partial_rows = jnp.dot(units, down_rows, preferred_element_type=jnp.float32)
            return (accumulated + partial_rows, None)
        expert_out, _ = lax.scan(add_units, jnp.zeros((row_block.shape[0], D), jnp.float32), jnp.arange(N_DP, dtype=jnp.int32))
        expert_out = expert_out.reshape(MICRO, N_DP, CAP, D)
        placed = jnp.einsum('mgct,mgcf->mgtf', dispatch_float, expert_out, precision=lax.Precision.HIGHEST)
        weight = expert_weight(expert_ids, first_gate, second_gate, expert).reshape(MICRO, N_DP, TOK_DEV, 1)
        return (summed + weight * placed, None)
    summed, _ = lax.scan(add_expert, jnp.zeros((MICRO, N_DP, TOK_DEV, D), jnp.float32), jnp.arange(EXPERTS, dtype=jnp.int32))
    return (widened + summed.reshape(MICRO, TOKENS, D)).astype(jnp.bfloat16)
```

```python
import functools

import jax
import jax.numpy as jnp
from jax import lax
from jax.experimental import pallas as pl
from jax.experimental.pallas import tpu as pltpu
from jax.sharding import PartitionSpec as P

epsilon = 1e-05
F32 = jnp.float32
BF16 = jnp.bfloat16
VMEM_LIMIT = 56 * 1024 * 1024


def exchange(array, axis, distance):
    count = lax.axis_size(axis)
    return lax.ppermute(array, axis, [(i, i ^ distance) for i in range(count)])


def chunk_rows(slot_total):
    units = slot_total // 16
    first = (units + 1) // 2
    return (first * 16, (units - first) * 16)


def route_kernel(rows, slots, expert_count, chunks, *refs):
    me, tokens_ref, gain_ref, router_ref, ids_ref, ids_row_ref = refs[:6]
    routed_refs, gates_ref = refs[6:-1], refs[-1]
    token_count = tokens_ref.shape[0]
    widened = tokens_ref[...].astype(F32)
    inverse_rms = lax.rsqrt(jnp.mean(widened * widened, axis=-1, keepdims=True) + epsilon)
    normed = (widened * inverse_rms * gain_ref[...].astype(F32)).astype(BF16)
    chosen = jnp.any(ids_row_ref[...] == me[0], axis=0, keepdims=True)
    earlier = lax.broadcasted_iota(jnp.int32, (token_count, token_count), 0)
    later = lax.broadcasted_iota(jnp.int32, (token_count, token_count), 1)
    same = lax.div(earlier, rows) == lax.div(later, rows)
    before = jnp.where((earlier < later) & same, 1.0, 0.0).astype(BF16)
    hits = jnp.where(chosen, 1.0, 0.0).astype(BF16)
    position = jnp.dot(
        jnp.broadcast_to(hits, (16, token_count)), before, preferred_element_type=F32
    )[0:1].astype(jnp.int32)
    token = lax.broadcasted_iota(jnp.int32, (1, token_count), 1)
    slot = lax.div(token, rows) * slots + position
    start = 0
    for routed_ref, size in zip(routed_refs, chunks):
        wanted = lax.broadcasted_iota(jnp.int32, (size, token_count), 0) + start
        dispatch = jnp.where((wanted == slot) & chosen, 1.0, 0.0).astype(BF16)
        routed_ref[...] = jnp.dot(dispatch, normed, preferred_element_type=F32).astype(BF16)
        start += size
    logits = lax.dot_general(
        normed, router_ref[...], (((1,), (1,)), ((), ())), preferred_element_type=F32
    )
    expert = lax.broadcasted_iota(jnp.int32, (token_count, expert_count), 1)
    first = jnp.sum(jnp.where(ids_ref[:, 0:1] == expert, logits, 0.0), axis=-1, keepdims=True)
    second = jnp.sum(jnp.where(ids_ref[:, 1:2] == expert, logits, 0.0), axis=-1, keepdims=True)
    gates_ref[:, 0:1] = jax.nn.sigmoid(first - second)
    gates_ref[:, 1:2] = jax.nn.sigmoid(second - first)


def route(me, tokens, norm_gain, router_weight, ids, rows, slots, chunks):
    token_count, width = tokens.shape
    expert_count = router_weight.shape[1]
    vmem = pl.BlockSpec(memory_space=pltpu.VMEM)
    out = pl.pallas_call(
        functools.partial(route_kernel, rows, slots, expert_count, chunks),
        out_shape=tuple(jax.ShapeDtypeStruct((c, width), BF16) for c in chunks)
        + (jax.ShapeDtypeStruct((token_count, 2), F32),),
        in_specs=[pl.BlockSpec(memory_space=pltpu.SMEM)] + [vmem] * 5,
        out_specs=(vmem,) * (len(chunks) + 1),
        compiler_params=pltpu.CompilerParams(vmem_limit_bytes=VMEM_LIMIT),
        name="route",
    )(me, tokens, norm_gain.reshape(1, width), router_weight.T, ids, ids.T)
    return out[:-1], out[-1]


def expert_kernel(block_count, up_steps, tile, *refs):
    blocks = refs[:block_count]
    gate_ref, up_ref, down_ref, kept_ref, sent_ref, rows_ref, hidden_ref, sems = refs[block_count:]
    size = blocks[0].shape[0]
    half = block_count // 2 * size
    step = pl.program_id(0)

    @pl.when(step == 0)
    def _():
        copies = [
            pltpu.make_async_copy(b, rows_ref.at[pl.ds(i * size, size)], sems.at[i])
            for i, b in enumerate(blocks)
        ]
        for c in copies:
            c.start()
        for c in copies:
            c.wait()

    @pl.when(step < up_steps)
    def _():
        gate = jnp.dot(rows_ref[...], gate_ref[...], preferred_element_type=F32)
        up = jnp.dot(rows_ref[...], up_ref[...], preferred_element_type=F32)
        hidden = gate / (1.0 + jnp.exp(-gate)) * up
        hidden_ref[:, pl.ds(pl.multiple_of(step * tile, tile), tile)] = hidden.astype(BF16)

    @pl.when(step >= up_steps)
    def _():
        out = jnp.dot(hidden_ref[...], down_ref[...], preferred_element_type=F32)
        kept_ref[...] = out[:half]
        sent_ref[...] = out[half:].astype(BF16)


def expert(blocks, gate_matrix, up_matrix, down_matrix):
    count, (size, width) = len(blocks), blocks[0].shape
    units = gate_matrix.shape[1]
    rows = count * size
    tile, down_tile = 256, 1024
    up_steps, down_steps = units // tile, width // down_tile
    up_spec = pl.BlockSpec((width, tile), lambda i: (0, jnp.minimum(i, up_steps - 1)))
    down_index = lambda i: (0, jnp.maximum(i - up_steps, 0))
    return pl.pallas_call(
        functools.partial(expert_kernel, count, up_steps, tile),
        out_shape=(
            jax.ShapeDtypeStruct((rows // 2, width), F32),
            jax.ShapeDtypeStruct((rows // 2, width), BF16),
        ),
        grid=(up_steps + down_steps,),
        in_specs=[pl.BlockSpec(memory_space=pl.ANY)] * count
        + [up_spec, up_spec, pl.BlockSpec((units, down_tile), down_index)],
        out_specs=(
            pl.BlockSpec((rows // 2, down_tile), down_index),
            pl.BlockSpec((rows // 2, down_tile), down_index),
        ),
        scratch_shapes=[
            pltpu.VMEM((rows, width), BF16),
            pltpu.VMEM((rows, units), BF16),
            pltpu.SemaphoreType.DMA((count,)),
        ],
        cost_estimate=pl.CostEstimate(
            flops=6 * rows * width * units,
            bytes_accessed=6 * width * units + 5 * rows * width,
            transcendentals=rows * units,
        ),
        compiler_params=pltpu.CompilerParams(vmem_limit_bytes=VMEM_LIMIT),
        name="expert",
    )(*blocks, gate_matrix, up_matrix, down_matrix)


def combine_kernel(rows, slots, count, chunks, *refs):
    me, own_ref, ids_ref, gates_ref = refs[:4]
    taken_refs, out_ref = refs[4:-1], refs[-1]
    token_count = own_ref.shape[0]
    later = lax.broadcasted_iota(jnp.int32, (token_count, token_count), 0)
    earlier = lax.broadcasted_iota(jnp.int32, (token_count, token_count), 1)
    same = lax.div(earlier, rows) == lax.div(later, rows)
    before = jnp.where((earlier < later) & same, 1.0, 0.0).astype(BF16)
    token = lax.broadcasted_iota(jnp.int32, (token_count, 1), 0)
    total = own_ref[...].astype(F32)
    for k in range(count):
        which = me[0] ^ k
        first, second = ids_ref[:, 0:1] == which, ids_ref[:, 1:2] == which
        chosen = first | second
        hits = jnp.where(chosen, 1.0, 0.0).astype(BF16)
        position = jnp.dot(
            before, jnp.broadcast_to(hits, (token_count, 128)), preferred_element_type=F32
        )[:, 0:1].astype(jnp.int32)
        slot = lax.div(token, rows) * slots + position
        weight = jnp.where(first, gates_ref[:, 0:1], 0.0) + jnp.where(
            second, gates_ref[:, 1:2], 0.0
        )
        start, placed = 0, None
        for c, size in enumerate(chunks):
            held = lax.broadcasted_iota(jnp.int32, (token_count, size), 1) + start
            pick = jnp.where((held == slot) & chosen, 1.0, 0.0).astype(BF16)
            part = jnp.dot(pick, taken_refs[c * count + k][...], preferred_element_type=F32)
            placed = part if placed is None else placed + part
            start += size
        total += weight * placed
    out_ref[...] = total.astype(BF16)


def combine(me, own, ids, gates, taken, rows, slots, chunks):
    count = len(taken) // len(chunks)
    vmem = pl.BlockSpec(memory_space=pltpu.VMEM)
    return pl.pallas_call(
        functools.partial(combine_kernel, rows, slots, count, chunks),
        out_shape=jax.ShapeDtypeStruct(own.shape, BF16),
        in_specs=[pl.BlockSpec(memory_space=pltpu.SMEM)] + [vmem] * (3 + len(taken)),
        out_specs=vmem,
        compiler_params=pltpu.CompilerParams(vmem_limit_bytes=VMEM_LIMIT),
        name="combine",
    )(me, own, ids, gates, *taken)


def gather_blocks(own, bits):
    held = {0: own}
    if len(bits) == 2:
        a, b = bits
        half = own.shape[0] // 2
        held[a], held[b] = exchange(own, "dp", a), exchange(own, "dp", b)
        low, high = exchange(held[b][:half], "dp", a), exchange(held[a][half:], "dp", b)
        return held, (low, high)
    for bit in bits:
        held.update({k | bit: exchange(v, "dp", bit) for k, v in list(held.items())})
    return held, None


def reduce_lane(terms, bits):
    terms = dict(terms)
    for bit in bits:
        leaving = sorted(k for k in terms if k & bit)
        outgoing = jnp.stack([sum(t.astype(F32) for t in terms[k]).astype(BF16) for k in leaving])
        incoming = exchange(outgoing, "dp", bit)
        for i, k in enumerate(leaving):
            terms[k ^ bit] = terms[k ^ bit] + [incoming[i]]
            del terms[k]
    return sum(t.astype(F32) for t in terms[0])


def per_device(tokens, norm_gain, router_weight, expert_ids, w_gate, w_up, w_down):
    micro_count, rows, width = tokens.shape
    expert_count = router_weight.shape[1]
    slots = 2 * rows // expert_count + rows // 8
    segment_count = lax.axis_size("segment")
    segment = lax.axis_index("segment")
    me = segment.astype(jnp.int32).reshape(1)
    bits = []
    while 2 ** (len(bits) + 1) < lax.axis_size("dp"):
        bits.append(2 ** (len(bits) + 1))
    slice_width = width // segment_count
    chunks = chunk_rows(micro_count * slots)
    flat = tokens.reshape(-1, width)
    ids = expert_ids.reshape(-1, 2)
    own_part = lax.dynamic_slice_in_dim(flat, segment * slice_width, slice_width, 1)
    routed, gates = route(me, flat, norm_gain, router_weight, ids, rows, slots, chunks)
    taken = []
    for own in routed:
        size = own.shape[0]
        held, halves = gather_blocks(own, bits)
        if halves is not None:
            held[bits[0] | bits[1]] = jnp.concatenate(halves)
        order = sorted(held)
        blocks = [held[k] for k in order]
        blocks = blocks + [exchange(b, "dp", 1) for b in blocks]
        kept, sent = expert(blocks, w_gate[0], w_up[0], w_down[0])
        partner = exchange(sent, "dp", 1)
        lanes = []
        for lane, lane_bits in enumerate((bits, bits[::-1])):
            columns = slice(lane * width // 2, (lane + 1) * width // 2)
            terms = {
                k: [a[i * size : (i + 1) * size, columns] for a in (kept, partner)]
                for i, k in enumerate(order)
            }
            lanes.append(reduce_lane(terms, lane_bits))
        total = jnp.concatenate(lanes, axis=1).astype(BF16)
        for k in range(segment_count):
            part = lax.dynamic_slice_in_dim(
                total, (segment ^ k) * slice_width, slice_width, 1
            )
            taken.append(part if k == 0 else exchange(part, "segment", k))
    out = combine(me, own_part, ids, gates, taken, rows, slots, chunks)
    return out.reshape(micro_count, rows, slice_width)


def solution(mesh):
    placed = (
        P(None, "dp", None),
        P(),
        P(),
        P(None, "dp", None),
        P("segment", None, "dp"),
        P("segment", None, "dp"),
        P("segment", "dp", None),
    )
    return jax.shard_map(
        per_device, mesh=mesh, in_specs=placed, out_specs=P(None, "dp", "segment"), check_vma=False
    )
```

```python
import functools

import jax
import jax.numpy as jnp
from jax import lax
from jax.experimental import pallas as pl
from jax.experimental.pallas import tpu as pltpu
from jax.sharding import PartitionSpec as P

epsilon = 1e-05
F32 = jnp.float32
BF16 = jnp.bfloat16
VMEM_LIMIT = 16 * 1024 * 1024
EXPERT_VMEM = 48 * 1024 * 1024


def exchange(array, axis, distance):
    count = lax.axis_size(axis)
    return lax.ppermute(array, axis, [(i, i ^ distance) for i in range(count)])


def chunk_rows(slot_total):
    units = slot_total // 16
    first = (units + 1) // 2
    return 16 * ((first + 1) // 2), 16 * (first // 2), 16 * (units - first)


def route_kernel(rows, slots, expert_count, chunks, *refs):
    me, tokens_ref, gain_ref, router_ref, ids_ref, ids_row_ref = refs[:6]
    routed_refs, gates_ref = refs[6:-1], refs[-1]
    token_count = tokens_ref.shape[0]
    widened = tokens_ref[...].astype(F32)
    inverse_rms = lax.rsqrt(jnp.mean(widened * widened, axis=-1, keepdims=True) + epsilon)
    normed = (widened * inverse_rms * gain_ref[...].astype(F32)).astype(BF16)
    chosen = jnp.any(ids_row_ref[...] == me[0], axis=0, keepdims=True)
    earlier = lax.broadcasted_iota(jnp.int32, (token_count, token_count), 0)
    later = lax.broadcasted_iota(jnp.int32, (token_count, token_count), 1)
    same = lax.div(earlier, rows) == lax.div(later, rows)
    before = jnp.where((earlier < later) & same, 1.0, 0.0).astype(BF16)
    hits = jnp.where(chosen, 1.0, 0.0).astype(BF16)
    position = jnp.dot(
        jnp.broadcast_to(hits, (16, token_count)), before, preferred_element_type=F32
    )[0:1].astype(jnp.int32)
    token = lax.broadcasted_iota(jnp.int32, (1, token_count), 1)
    slot = lax.div(token, rows) * slots + position
    start = 0
    for routed_ref, size in zip(routed_refs, chunks):
        wanted = lax.broadcasted_iota(jnp.int32, (size, token_count), 0) + start
        dispatch = jnp.where((wanted == slot) & chosen, 1.0, 0.0).astype(BF16)
        routed_ref[...] = jnp.dot(dispatch, normed, preferred_element_type=F32).astype(BF16)
        start += size
    logits = lax.dot_general(
        normed, router_ref[...], (((1,), (1,)), ((), ())), preferred_element_type=F32
    )
    expert = lax.broadcasted_iota(jnp.int32, (token_count, expert_count), 1)
    first = jnp.sum(jnp.where(ids_ref[:, 0:1] == expert, logits, 0.0), axis=-1, keepdims=True)
    second = jnp.sum(jnp.where(ids_ref[:, 1:2] == expert, logits, 0.0), axis=-1, keepdims=True)
    gates_ref[:, 0:1] = jax.nn.sigmoid(first - second)
    gates_ref[:, 1:2] = jax.nn.sigmoid(second - first)


def route(me, tokens, norm_gain, router_weight, ids, rows, slots, chunks):
    token_count, width = tokens.shape
    expert_count = router_weight.shape[1]
    vmem = pl.BlockSpec(memory_space=pltpu.VMEM)
    out = pl.pallas_call(
        functools.partial(route_kernel, rows, slots, expert_count, chunks),
        out_shape=tuple(jax.ShapeDtypeStruct((c, width), BF16) for c in chunks)
        + (jax.ShapeDtypeStruct((token_count, 2), F32),),
        in_specs=[pl.BlockSpec(memory_space=pltpu.SMEM)] + [vmem] * 5,
        out_specs=(vmem,) * (len(chunks) + 1),
        compiler_params=pltpu.CompilerParams(vmem_limit_bytes=VMEM_LIMIT),
        name="route",
    )(me, tokens, norm_gain.reshape(1, width), router_weight.T, ids, ids.T)
    return out[:-1], out[-1]


def staged(fetches, ahead):
    def arrive(n):
        for c in fetches[n]:
            c.wait()
        if n + ahead < len(fetches):
            for c in fetches[n + ahead]:
                c.start()

    for c in [c for group in fetches[:ahead] for c in group]:
        c.start()
    return arrive


def up_kernel(block_count, *refs):
    blocks, refs = refs[:block_count], refs[block_count:]
    gate_ref, up_ref, hidden_ref, rows_ref, held_ref, sems, held_sems = refs
    buffers, _, _, tile = held_ref.shape
    copies, start = [], 0
    for i, block in enumerate(blocks):
        target = rows_ref.at[pl.ds(start, block.shape[0])]
        copies.append(pltpu.make_async_copy(block, target, sems.at[i]))
        start += block.shape[0]
    for c in copies:
        c.start()
    fetches = []
    for j in range(gate_ref.shape[1] // tile):
        part, slot = pl.ds(j * tile, tile), j % buffers
        fetches.append(
            [
                pltpu.make_async_copy(r.at[:, part], held_ref.at[slot, i], held_sems.at[slot, i])
                for i, r in enumerate((gate_ref, up_ref))
            ]
        )
    arrive = staged(fetches, 2)
    for c in copies:
        c.wait()
    for j in range(len(fetches)):
        arrive(j)
        gate = jnp.dot(rows_ref[...], held_ref[j % buffers, 0], preferred_element_type=F32)
        up = jnp.dot(rows_ref[...], held_ref[j % buffers, 1], preferred_element_type=F32)
        hidden = gate / (1.0 + jnp.exp(-gate)) * up
        hidden_ref[:, j * tile : (j + 1) * tile] = hidden.astype(BF16)


def up_projection(blocks, gate_matrix, up_matrix):
    rows, (width, units) = sum(b.shape[0] for b in blocks), gate_matrix.shape
    buffers, tile = 3, 256
    return pl.pallas_call(
        functools.partial(up_kernel, len(blocks)),
        out_shape=jax.ShapeDtypeStruct((rows, units), BF16),
        in_specs=[pl.BlockSpec(memory_space=pl.ANY)] * (len(blocks) + 2),
        out_specs=pl.BlockSpec(memory_space=pltpu.VMEM),
        scratch_shapes=[
            pltpu.VMEM((rows, width), BF16),
            pltpu.VMEM((buffers, 2, width, tile), BF16),
            pltpu.SemaphoreType.DMA((len(blocks),)),
            pltpu.SemaphoreType.DMA((buffers, 2)),
        ],
        cost_estimate=pl.CostEstimate(
            flops=4 * rows * width * units,
            bytes_accessed=4 * width * units + 2 * rows * width,
            transcendentals=rows * units,
        ),
        compiler_params=pltpu.CompilerParams(vmem_limit_bytes=EXPERT_VMEM),
        name="up",
    )(*blocks, gate_matrix, up_matrix)


def down_kernel(out_count, hidden_ref, down_ref, *refs):
    out_refs, (held_ref, held_sems) = refs[:out_count], refs[out_count:]
    buffers, _, tile = held_ref.shape
    size = hidden_ref.shape[0] // out_count
    fetches = []
    for j in range(down_ref.shape[1] // tile):
        part, slot = pl.ds(j * tile, tile), j % buffers
        fetches.append(
            [pltpu.make_async_copy(down_ref.at[:, part], held_ref.at[slot], held_sems.at[slot])]
        )
    arrive = staged(fetches, 2)
    for j in range(len(fetches)):
        arrive(j)
        part = slice(j * tile, (j + 1) * tile)
        out = jnp.dot(hidden_ref[...], held_ref[j % buffers], preferred_element_type=F32)
        for i, out_ref in enumerate(out_refs):
            out_ref[:, part] = out[i * size : (i + 1) * size].astype(out_ref.dtype)


def down_projection(hidden, count, down_matrix):
    rows, (units, width) = hidden.shape[0], down_matrix.shape
    buffers, tile = 3, width // 4
    vmem = pl.BlockSpec(memory_space=pltpu.VMEM)
    out = pl.pallas_call(
        functools.partial(down_kernel, count),
        out_shape=tuple(
            jax.ShapeDtypeStruct((rows // count, width), F32 if i < count // 2 else BF16)
            for i in range(count)
        ),
        in_specs=[vmem, pl.BlockSpec(memory_space=pl.ANY)],
        out_specs=(vmem,) * count,
        scratch_shapes=[
            pltpu.VMEM((buffers, units, tile), BF16),
            pltpu.SemaphoreType.DMA((buffers,)),
        ],
        cost_estimate=pl.CostEstimate(
            flops=2 * rows * width * units,
            bytes_accessed=2 * width * units + 3 * rows * width,
            transcendentals=0,
        ),
        compiler_params=pltpu.CompilerParams(vmem_limit_bytes=EXPERT_VMEM),
        name="down",
    )(hidden, down_matrix)
    return out[: count // 2], out[count // 2 :]


def combine_kernel(rows, slots, count, chunks, *refs):
    me, own_ref, ids_ref, gates_ref = refs[:4]
    taken_refs, out_ref = refs[4:-1], refs[-1]
    token_count = own_ref.shape[0]
    later = lax.broadcasted_iota(jnp.int32, (token_count, token_count), 0)
    earlier = lax.broadcasted_iota(jnp.int32, (token_count, token_count), 1)
    same = lax.div(earlier, rows) == lax.div(later, rows)
    before = jnp.where((earlier < later) & same, 1.0, 0.0).astype(BF16)
    token = lax.broadcasted_iota(jnp.int32, (token_count, 1), 0)
    total = own_ref[...].astype(F32)
    for k in range(count):
        which = me[0] ^ k
        first, second = ids_ref[:, 0:1] == which, ids_ref[:, 1:2] == which
        chosen = first | second
        hits = jnp.where(chosen, 1.0, 0.0).astype(BF16)
        position = jnp.dot(
            before, jnp.broadcast_to(hits, (token_count, 128)), preferred_element_type=F32
        )[:, 0:1].astype(jnp.int32)
        slot = lax.div(token, rows) * slots + position
        weight = jnp.where(first, gates_ref[:, 0:1], 0.0) + jnp.where(
            second, gates_ref[:, 1:2], 0.0
        )
        start, placed = 0, None
        for c, size in enumerate(chunks):
            held = lax.broadcasted_iota(jnp.int32, (token_count, size), 1) + start
            pick = jnp.where((held == slot) & chosen, 1.0, 0.0).astype(BF16)
            part = jnp.dot(pick, taken_refs[c * count + k][...], preferred_element_type=F32)
            placed = part if placed is None else placed + part
            start += size
        total += weight * placed
    out_ref[...] = total.astype(BF16)


def combine(me, own, ids, gates, taken, rows, slots, chunks):
    count = len(taken) // len(chunks)
    vmem = pl.BlockSpec(memory_space=pltpu.VMEM)
    return pl.pallas_call(
        functools.partial(combine_kernel, rows, slots, count, chunks),
        out_shape=jax.ShapeDtypeStruct(own.shape, BF16),
        in_specs=[pl.BlockSpec(memory_space=pltpu.SMEM)] + [vmem] * (3 + len(taken)),
        out_specs=vmem,
        compiler_params=pltpu.CompilerParams(vmem_limit_bytes=VMEM_LIMIT),
        name="combine",
    )(me, own, ids, gates, *taken)


def together(*groups):
    flat = lax.optimization_barrier([a for g in groups for a in g])
    return [[flat.pop(0) for _ in g] for g in groups]


def after(array, *earlier):
    return lax.optimization_barrier((array, *earlier))[0]


class Chunk:
    def __init__(self, pieces, bits):
        self.own, self.bits = pieces, bits

    def spread(self):
        self.held = {0: self.own}
        if len(self.bits) == 2:
            for bit in self.bits:
                self.held[bit] = [exchange(p, "dp", bit) for p in self.own]
        else:
            for bit in self.bits:
                for k, v in list(self.held.items()):
                    self.held[k | bit] = [exchange(p, "dp", bit) for p in v]

    def forward(self):
        if len(self.bits) == 2:
            a, b = self.bits
            last = []
            for i, (source, bit) in enumerate(((b, a), (a, b))):
                pieces = self.held[source]
                if len(pieces) == 1:
                    half = pieces[0].shape[0] // 2
                    pieces = [pieces[0][:half], pieces[0][half:]]
                last.append(exchange(pieces[i], "dp", bit))
            self.held[a | b] = last

    def up(self, matrices, *earlier):
        self.order = sorted(self.held)
        blocks = [p for k in self.order for p in self.held[k]]
        blocks = blocks + [exchange(block, "dp", 1) for block in blocks]
        if earlier:
            blocks[0] = after(blocks[0], *earlier)
        self.hidden = up_projection(blocks, *matrices[:2])

    def down(self, matrices):
        self.kept, self.sent = down_projection(self.hidden, 2 * len(self.order), matrices[2])

    def pair_sum(self):
        partner = [exchange(sent, "dp", 1) for sent in self.sent]
        width = self.own[0].shape[1]
        self.lanes = []
        for lane, bits in enumerate((self.bits, self.bits[::-1])):
            columns = slice(lane * width // 2, (lane + 1) * width // 2)
            terms = {
                k: [kept[:, columns], other[:, columns]]
                for k, kept, other in zip(self.order, self.kept, partner)
            }
            self.lanes.append((terms, bits))

    def leave(self, step):
        self.outgoing = []
        for terms, bits in self.lanes:
            leaving = sorted(k for k in terms if k & bits[step])
            self.outgoing.append(
                jnp.stack([sum(t.astype(F32) for t in terms[k]).astype(BF16) for k in leaving])
            )
        return self.outgoing

    def send(self, step):
        self.incoming = [
            exchange(out, "dp", bits[step]) for out, (_, bits) in zip(self.outgoing, self.lanes)
        ]

    def arrive(self, step):
        for incoming, (terms, bits) in zip(self.incoming, self.lanes):
            for i, k in enumerate(sorted(k for k in terms if k & bits[step])):
                terms[k ^ bits[step]] = terms[k ^ bits[step]] + [incoming[i]]
                del terms[k]

    def finish(self):
        sums = [sum(t.astype(F32) for t in terms[0]) for terms, _ in self.lanes]
        total = jnp.concatenate(sums, axis=1).astype(BF16)
        count, segment = lax.axis_size("segment"), lax.axis_index("segment")
        width = total.shape[1] // count
        parts = [
            lax.dynamic_slice_in_dim(total, (segment ^ k) * width, width, 1) for k in range(count)
        ]
        return [parts[0]] + [exchange(parts[k], "segment", k) for k in range(1, count)]


def per_device(tokens, norm_gain, router_weight, expert_ids, w_gate, w_up, w_down):
    micro_count, rows, width = tokens.shape
    expert_count = router_weight.shape[1]
    slots = 2 * rows // expert_count + rows // 8
    segment_count = lax.axis_size("segment")
    segment = lax.axis_index("segment")
    me = segment.astype(jnp.int32).reshape(1)
    bits = []
    while 2 ** (len(bits) + 1) < lax.axis_size("dp"):
        bits.append(2 ** (len(bits) + 1))
    slice_width = width // segment_count
    sizes = chunk_rows(micro_count * slots)
    flat = tokens.reshape(-1, width)
    ids = expert_ids.reshape(-1, 2)
    own_part = lax.dynamic_slice_in_dim(flat, segment * slice_width, slice_width, 1)
    routed, gates = route(me, flat, norm_gain, router_weight, ids, rows, slots, sizes)
    matrices = w_gate[0], w_up[0], w_down[0]
    one, two = Chunk(routed[:2], bits), Chunk(routed[2:], bits)
    one.spread()
    two.own = [after(p, *(p for b in bits for p in one.held[b])) for p in two.own]
    two.spread()
    one.forward()
    one.up(matrices)
    hops = [b for b in sorted(two.held) if b]
    (one.hidden,), *arrived = together([one.hidden], *(two.held[b] for b in hops))
    two.held.update(zip(hops, arrived))
    two.forward()
    one.down(matrices)
    last = max(two.held)
    one.kept, one.sent, two.held[last] = together(one.kept, one.sent, two.held[last])
    one.pair_sum()
    steps = len(bits)
    one.leave(0)
    one.send(0)
    two.up(matrices, *one.outgoing)
    (two.hidden,), one.incoming = together([two.hidden], one.incoming)
    one.arrive(0)
    for step in range(1, steps):
        one.leave(step)
        one.send(step)
        if step < steps - 1:
            one.arrive(step)
    two.down(matrices)
    two.kept, two.sent, one.incoming = together(two.kept, two.sent, one.incoming)
    one.arrive(steps - 1)
    two.pair_sum()
    two.leave(0)
    two.send(0)
    taken = one.finish()
    taken[1:], two.incoming = together(taken[1:], two.incoming)
    two.arrive(0)
    for step in range(1, steps):
        two.leave(step)
        two.send(step)
        two.arrive(step)
    taken = taken + two.finish()
    wholes = sum(sizes[:2]), sizes[2]
    out = combine(me, own_part, ids, gates, taken, rows, slots, wholes)
    return out.reshape(micro_count, rows, slice_width)


def solution(mesh):
    placed = (
        P(None, "dp", None),
        P(),
        P(),
        P(None, "dp", None),
        P("segment", None, "dp"),
        P("segment", None, "dp"),
        P("segment", "dp", None),
    )
    return jax.shard_map(
        per_device, mesh=mesh, in_specs=placed, out_specs=P(None, "dp", "segment"), check_vma=False
    )
```

```python
import functools

import jax
import jax.numpy as jnp
from jax import lax
from jax.experimental import pallas as pl
from jax.experimental.pallas import tpu as pltpu
from jax.sharding import PartitionSpec as P

epsilon = 1e-05
F32 = jnp.float32
BF16 = jnp.bfloat16
VMEM_LIMIT = 16 * 1024 * 1024
EXPERT_VMEM = 40 * 1024 * 1024
DOWN_VMEM = 28 * 1024 * 1024


def exchange(array, axis, distance):
    count = lax.axis_size(axis)
    return lax.ppermute(array, axis, [(i, i ^ distance) for i in range(count)])


def chunk_rows(slot_total):
    units = slot_total // 16
    first = (units + 1) // 2
    return 16 * first, 16 * (units - first)


def route_kernel(rows, slots, expert_count, chunks, *refs):
    me, tokens_ref, gain_ref, router_ref, ids_ref, ids_row_ref = refs[:6]
    routed_refs, gates_ref = refs[6:-1], refs[-1]
    token_count = tokens_ref.shape[0]
    widened = tokens_ref[...].astype(F32)
    inverse_rms = lax.rsqrt(jnp.mean(widened * widened, axis=-1, keepdims=True) + epsilon)
    normed = (widened * inverse_rms * gain_ref[...].astype(F32)).astype(BF16)
    chosen = jnp.any(ids_row_ref[...] == me[0], axis=0, keepdims=True)
    earlier = lax.broadcasted_iota(jnp.int32, (token_count, token_count), 0)
    later = lax.broadcasted_iota(jnp.int32, (token_count, token_count), 1)
    same = lax.div(earlier, rows) == lax.div(later, rows)
    before = jnp.where((earlier < later) & same, 1.0, 0.0).astype(BF16)
    hits = jnp.where(chosen, 1.0, 0.0).astype(BF16)
    position = jnp.dot(
        jnp.broadcast_to(hits, (16, token_count)), before, preferred_element_type=F32
    )[0:1].astype(jnp.int32)
    token = lax.broadcasted_iota(jnp.int32, (1, token_count), 1)
    slot = lax.div(token, rows) * slots + position
    start = 0
    for routed_ref, size in zip(routed_refs, chunks):
        wanted = lax.broadcasted_iota(jnp.int32, (size, token_count), 0) + start
        dispatch = jnp.where((wanted == slot) & chosen, 1.0, 0.0).astype(BF16)
        routed_ref[...] = jnp.dot(dispatch, normed, preferred_element_type=F32).astype(BF16)
        start += size
    logits = lax.dot_general(
        normed, router_ref[...], (((1,), (1,)), ((), ())), preferred_element_type=F32
    )
    expert = lax.broadcasted_iota(jnp.int32, (token_count, expert_count), 1)
    first = jnp.sum(jnp.where(ids_ref[:, 0:1] == expert, logits, 0.0), axis=-1, keepdims=True)
    second = jnp.sum(jnp.where(ids_ref[:, 1:2] == expert, logits, 0.0), axis=-1, keepdims=True)
    gates_ref[:, 0:1] = jax.nn.sigmoid(first - second)
    gates_ref[:, 1:2] = jax.nn.sigmoid(second - first)


def route(me, tokens, norm_gain, router_weight, ids, rows, slots, chunks):
    token_count, width = tokens.shape
    expert_count = router_weight.shape[1]
    vmem = pl.BlockSpec(memory_space=pltpu.VMEM)
    out = pl.pallas_call(
        functools.partial(route_kernel, rows, slots, expert_count, chunks),
        out_shape=tuple(jax.ShapeDtypeStruct((c, width), BF16) for c in chunks)
        + (jax.ShapeDtypeStruct((token_count, 2), F32),),
        in_specs=[pl.BlockSpec(memory_space=pltpu.SMEM)] + [vmem] * 5,
        out_specs=(vmem,) * (len(chunks) + 1),
        compiler_params=pltpu.CompilerParams(vmem_limit_bytes=VMEM_LIMIT),
        name="route",
    )(me, tokens, norm_gain.reshape(1, width), router_weight.T, ids, ids.T)
    return out[:-1], out[-1]


def staged(fetches, ahead):
    def arrive(n):
        for c in fetches[n]:
            c.wait()
        if n + ahead < len(fetches):
            for c in fetches[n + ahead]:
                c.start()

    for c in [c for group in fetches[:ahead] for c in group]:
        c.start()
    return arrive


def up_kernel(block_count, *refs):
    blocks, refs = refs[:block_count], refs[block_count:]
    gate_ref, up_ref, hidden_ref, rows_ref, held_ref, sems, held_sems = refs
    buffers, _, _, tile = held_ref.shape
    copies, start, column = [], 0, 0
    for i, block in enumerate(blocks):
        size, part = block.shape
        target = rows_ref.at[pl.ds(start, size), pl.ds(column, part)]
        copies.append(pltpu.make_async_copy(block, target, sems.at[i]))
        column += part
        if column == rows_ref.shape[1]:
            start, column = start + size, 0
    for c in copies:
        c.start()
    fetches = []
    for j in range(gate_ref.shape[1] // tile):
        part, slot = pl.ds(j * tile, tile), j % buffers
        fetches.append(
            [
                pltpu.make_async_copy(r.at[:, part], held_ref.at[slot, i], held_sems.at[slot, i])
                for i, r in enumerate((gate_ref, up_ref))
            ]
        )
    arrive = staged(fetches, 2)
    for c in copies:
        c.wait()
    for j in range(len(fetches)):
        arrive(j)
        gate = jnp.dot(rows_ref[...], held_ref[j % buffers, 0], preferred_element_type=F32)
        up = jnp.dot(rows_ref[...], held_ref[j % buffers, 1], preferred_element_type=F32)
        hidden = gate / (1.0 + jnp.exp(-gate)) * up
        hidden_ref[:, j * tile : (j + 1) * tile] = hidden.astype(BF16)


def up_projection(blocks, gate_matrix, up_matrix):
    width, units = gate_matrix.shape
    rows = sum(b.size for b in blocks) // width
    buffers, tile = 3, 256
    return pl.pallas_call(
        functools.partial(up_kernel, len(blocks)),
        out_shape=jax.ShapeDtypeStruct((rows, units), BF16),
        in_specs=[pl.BlockSpec(memory_space=pl.ANY)] * (len(blocks) + 2),
        out_specs=pl.BlockSpec(memory_space=pltpu.VMEM),
        scratch_shapes=[
            pltpu.VMEM((rows, width), BF16),
            pltpu.VMEM((buffers, 2, width, tile), BF16),
            pltpu.SemaphoreType.DMA((len(blocks),)),
            pltpu.SemaphoreType.DMA((buffers, 2)),
        ],
        cost_estimate=pl.CostEstimate(
            flops=4 * rows * width * units,
            bytes_accessed=4 * width * units + 2 * rows * width,
            transcendentals=rows * units,
        ),
        compiler_params=pltpu.CompilerParams(vmem_limit_bytes=EXPERT_VMEM),
        name="up",
    )(*blocks, gate_matrix, up_matrix)


def down_kernel(out_count, hidden_ref, down_ref, *refs):
    out_refs, (held_ref, held_sems) = refs[:out_count], refs[out_count:]
    buffers, _, tile = held_ref.shape
    size = hidden_ref.shape[0] // out_count
    fetches = []
    for j in range(down_ref.shape[1] // tile):
        part, slot = pl.ds(j * tile, tile), j % buffers
        fetches.append(
            [pltpu.make_async_copy(down_ref.at[:, part], held_ref.at[slot], held_sems.at[slot])]
        )
    arrive = staged(fetches, 2)
    for j in range(len(fetches)):
        arrive(j)
        part = slice(j * tile, (j + 1) * tile)
        out = jnp.dot(hidden_ref[...], held_ref[j % buffers], preferred_element_type=F32)
        for i, out_ref in enumerate(out_refs):
            out_ref[:, part] = out[i * size : (i + 1) * size].astype(out_ref.dtype)


def down_projection(hidden, count, down_matrix, place):
    rows, (units, width) = hidden.shape[0], down_matrix.shape
    buffers, tile = 3, width // 4
    vmem = pl.BlockSpec(memory_space=pltpu.VMEM)
    out = pl.pallas_call(
        functools.partial(down_kernel, count),
        out_shape=tuple(
            place((rows // count, width), F32 if i < count // 2 else BF16)
            for i in range(count)
        ),
        in_specs=[vmem, pl.BlockSpec(memory_space=pl.ANY)],
        out_specs=(vmem,) * count,
        scratch_shapes=[
            pltpu.VMEM((buffers, units, tile), BF16),
            pltpu.SemaphoreType.DMA((buffers,)),
        ],
        cost_estimate=pl.CostEstimate(
            flops=2 * rows * width * units,
            bytes_accessed=2 * width * units + 3 * rows * width,
            transcendentals=0,
        ),
        compiler_params=pltpu.CompilerParams(vmem_limit_bytes=DOWN_VMEM),
        name="down",
    )(hidden, down_matrix)
    return out[: count // 2], out[count // 2 :]


def combine_kernel(rows, slots, count, chunks, *refs):
    me, own_ref, ids_ref, gates_ref = refs[:4]
    taken_refs, out_ref = refs[4:-1], refs[-1]
    token_count = own_ref.shape[0]
    later = lax.broadcasted_iota(jnp.int32, (token_count, token_count), 0)
    earlier = lax.broadcasted_iota(jnp.int32, (token_count, token_count), 1)
    same = lax.div(earlier, rows) == lax.div(later, rows)
    before = jnp.where((earlier < later) & same, 1.0, 0.0).astype(BF16)
    token = lax.broadcasted_iota(jnp.int32, (token_count, 1), 0)
    total = own_ref[...].astype(F32)
    for k in range(count):
        which = me[0] ^ k
        first, second = ids_ref[:, 0:1] == which, ids_ref[:, 1:2] == which
        chosen = first | second
        hits = jnp.where(chosen, 1.0, 0.0).astype(BF16)
        position = jnp.dot(
            before, jnp.broadcast_to(hits, (token_count, 128)), preferred_element_type=F32
        )[:, 0:1].astype(jnp.int32)
        slot = lax.div(token, rows) * slots + position
        weight = jnp.where(first, gates_ref[:, 0:1], 0.0) + jnp.where(
            second, gates_ref[:, 1:2], 0.0
        )
        start, placed = 0, None
        for c, size in enumerate(chunks):
            held = lax.broadcasted_iota(jnp.int32, (token_count, size), 1) + start
            pick = jnp.where((held == slot) & chosen, 1.0, 0.0).astype(BF16)
            part = jnp.dot(pick, taken_refs[c * count + k][...], preferred_element_type=F32)
            placed = part if placed is None else placed + part
            start += size
        total += weight * placed
    out_ref[...] = total.astype(BF16)


def combine(me, own, ids, gates, taken, rows, slots, chunks):
    count = len(taken) // len(chunks)
    vmem = pl.BlockSpec(memory_space=pltpu.VMEM)
    return pl.pallas_call(
        functools.partial(combine_kernel, rows, slots, count, chunks),
        out_shape=jax.ShapeDtypeStruct(own.shape, BF16),
        in_specs=[pl.BlockSpec(memory_space=pltpu.SMEM)] + [vmem] * (3 + len(taken)),
        out_specs=vmem,
        compiler_params=pltpu.CompilerParams(vmem_limit_bytes=VMEM_LIMIT),
        name="combine",
    )(me, own, ids, gates, *taken)


def together(*groups):
    flat = lax.optimization_barrier([a for g in groups for a in g])
    return [[flat.pop(0) for _ in g] for g in groups]


def after(array, *earlier):
    return lax.optimization_barrier((array, *earlier))[0]


class Chunk:
    def __init__(self, own, bits):
        self.own, self.bits = own, bits

    def spread(self):
        self.held = {0: [self.own]}
        if len(self.bits) == 2:
            for bit in self.bits:
                self.held[bit] = [exchange(self.own, "dp", bit)]
        else:
            for bit in self.bits:
                for k, v in list(self.held.items()):
                    self.held[k | bit] = [exchange(p, "dp", bit) for p in v]

    def forward(self):
        if len(self.bits) == 2:
            a, b = self.bits
            half = self.own.shape[1] // 2
            left, right = self.held[b][0][:, :half], self.held[a][0][:, half:]
            self.held[a | b] = [exchange(left, "dp", a), exchange(right, "dp", b)]

    def up(self, matrices, *earlier):
        self.order = sorted(self.held)
        blocks = [p for k in self.order for p in self.held[k]]
        blocks = blocks + [exchange(block, "dp", 1) for block in blocks]
        if earlier:
            blocks[0] = after(blocks[0], *earlier)
        self.hidden = up_projection(blocks, *matrices[:2])

    def down(self, matrices, place):
        count = 2 * len(self.order)
        self.kept, self.sent = down_projection(self.hidden, count, matrices[2], place)

    def pair_sum(self):
        partner = [exchange(sent, "dp", 1) for sent in self.sent]
        width = self.own.shape[1]
        self.lanes = []
        for lane, bits in enumerate((self.bits, self.bits[::-1])):
            columns = slice(lane * width // 2, (lane + 1) * width // 2)
            terms = {
                k: [kept[:, columns], other[:, columns]]
                for k, kept, other in zip(self.order, self.kept, partner)
            }
            self.lanes.append((terms, bits))

    def leave(self, step):
        self.outgoing = []
        for terms, bits in self.lanes:
            leaving = sorted(k for k in terms if k & bits[step])
            self.outgoing.append(
                jnp.stack([sum(t.astype(F32) for t in terms[k]).astype(BF16) for k in leaving])
            )
        return self.outgoing

    def send(self, step):
        self.incoming = [
            exchange(out, "dp", bits[step]) for out, (_, bits) in zip(self.outgoing, self.lanes)
        ]

    def arrive(self, step):
        for incoming, (terms, bits) in zip(self.incoming, self.lanes):
            for i, k in enumerate(sorted(k for k in terms if k & bits[step])):
                terms[k ^ bits[step]] = terms[k ^ bits[step]] + [incoming[i]]
                del terms[k]

    def finish(self):
        sums = [sum(t.astype(F32) for t in terms[0]) for terms, _ in self.lanes]
        total = jnp.concatenate(sums, axis=1).astype(BF16)
        count, segment = lax.axis_size("segment"), lax.axis_index("segment")
        width = total.shape[1] // count
        parts = [
            lax.dynamic_slice_in_dim(total, (segment ^ k) * width, width, 1) for k in range(count)
        ]
        return [parts[0]] + [exchange(parts[k], "segment", k) for k in range(1, count)]


def per_device(tokens, norm_gain, router_weight, expert_ids, w_gate, w_up, w_down):
    micro_count, rows, width = tokens.shape
    expert_count = router_weight.shape[1]
    slots = 2 * rows // expert_count + rows // 8
    segment_count = lax.axis_size("segment")
    segment = lax.axis_index("segment")
    me = segment.astype(jnp.int32).reshape(1)
    bits = []
    while 2 ** (len(bits) + 1) < lax.axis_size("dp"):
        bits.append(2 ** (len(bits) + 1))
    slice_width = width // segment_count
    sizes = chunk_rows(micro_count * slots)
    flat = tokens.reshape(-1, width)
    ids = expert_ids.reshape(-1, 2)
    own_part = lax.dynamic_slice_in_dim(flat, segment * slice_width, slice_width, 1)
    routed, gates = route(me, flat, norm_gain, router_weight, ids, rows, slots, sizes)
    matrices = w_gate[0], w_up[0], w_down[0]
    one, two = (Chunk(own, bits) for own in routed)
    one.spread()
    two.own = after(two.own, *(p for b in bits for p in one.held[b]))
    two.spread()
    one.forward()
    one.up(matrices)
    hops = [b for b in sorted(two.held) if b]
    (one.hidden,), *arrived = together([one.hidden], *(two.held[b] for b in hops))
    two.held.update(zip(hops, arrived))
    two.forward()
    one.down(matrices, jax.ShapeDtypeStruct)
    last = max(two.held)
    one.kept, one.sent, two.held[last] = together(one.kept, one.sent, two.held[last])
    one.pair_sum()
    steps = len(bits)
    one.leave(0)
    one.send(0)
    two.up(matrices, *one.outgoing)
    (two.hidden,), one.incoming = together([two.hidden], one.incoming)
    one.arrive(0)
    for step in range(1, steps):
        one.leave(step)
        one.send(step)
        if step < steps - 1:
            one.arrive(step)
    two.down(matrices, pltpu.HBM)
    two.kept, two.sent, one.incoming = together(two.kept, two.sent, one.incoming)
    one.arrive(steps - 1)
    two.pair_sum()
    two.leave(0)
    two.send(0)
    taken = one.finish()
    for step in range(steps):
        if step < 1:
            share = slice(1, 3)
            taken[share], two.incoming = together(taken[share], two.incoming)
        two.arrive(step)
        if step + 1 < steps:
            two.leave(step + 1)
            two.send(step + 1)
    taken = taken + two.finish()
    out = combine(me, own_part, ids, gates, taken, rows, slots, sizes)
    return out.reshape(micro_count, rows, slice_width)


def solution(mesh):
    placed = (
        P(None, "dp", None),
        P(),
        P(),
        P(None, "dp", None),
        P("segment", None, "dp"),
        P("segment", None, "dp"),
        P("segment", "dp", None),
    )
    return jax.shard_map(
        per_device, mesh=mesh, in_specs=placed, out_specs=P(None, "dp", "segment"), check_vma=False
    )
```

```python
import functools

import jax
import jax.numpy as jnp
from jax import lax
from jax.experimental import pallas as pl
from jax.experimental.pallas import tpu as pltpu
from jax.sharding import PartitionSpec as P

epsilon = 1e-05
F32 = jnp.float32
BF16 = jnp.bfloat16
VMEM_LIMIT = 16 * 1024 * 1024
EXPERT_VMEM = 40 * 1024 * 1024
DOWN_VMEM = 28 * 1024 * 1024


def exchange(array, axis, distance):
    count = lax.axis_size(axis)
    return lax.ppermute(array, axis, [(i, i ^ distance) for i in range(count)])


def chunk_rows(slot_total):
    units = slot_total // 16
    first = (units + 1) // 2
    return 16 * first, 16 * (units - first)


def route_kernel(rows, slots, expert_count, chunks, *refs):
    me, tokens_ref, gain_ref, router_ref, ids_ref, ids_row_ref = refs[:6]
    routed_refs, (gates_ref, held_ref, sem) = refs[6:-3], refs[-3:]
    token_count = tokens_ref.shape[0]
    copy = pltpu.make_async_copy(tokens_ref, held_ref, sem)
    copy.start()
    copy.wait()
    widened = held_ref[...].astype(F32)
    inverse_rms = lax.rsqrt(jnp.mean(widened * widened, axis=-1, keepdims=True) + epsilon)
    normed = (widened * inverse_rms * gain_ref[...].astype(F32)).astype(BF16)
    chosen = jnp.any(ids_row_ref[...] == me[0], axis=0, keepdims=True)
    earlier = lax.broadcasted_iota(jnp.int32, (token_count, token_count), 0)
    later = lax.broadcasted_iota(jnp.int32, (token_count, token_count), 1)
    same = lax.div(earlier, rows) == lax.div(later, rows)
    before = jnp.where((earlier < later) & same, 1.0, 0.0).astype(BF16)
    hits = jnp.where(chosen, 1.0, 0.0).astype(BF16)
    position = jnp.dot(
        jnp.broadcast_to(hits, (16, token_count)), before, preferred_element_type=F32
    )[0:1].astype(jnp.int32)
    token = lax.broadcasted_iota(jnp.int32, (1, token_count), 1)
    slot = lax.div(token, rows) * slots + position
    start = 0
    for routed_ref, size in zip(routed_refs, chunks):
        wanted = lax.broadcasted_iota(jnp.int32, (size, token_count), 0) + start
        dispatch = jnp.where((wanted == slot) & chosen, 1.0, 0.0).astype(BF16)
        routed_ref[...] = jnp.dot(dispatch, normed, preferred_element_type=F32).astype(BF16)
        start += size
    logits = lax.dot_general(
        normed, router_ref[...], (((1,), (1,)), ((), ())), preferred_element_type=F32
    )
    expert = lax.broadcasted_iota(jnp.int32, (token_count, expert_count), 1)
    first = jnp.sum(jnp.where(ids_ref[:, 0:1] == expert, logits, 0.0), axis=-1, keepdims=True)
    second = jnp.sum(jnp.where(ids_ref[:, 1:2] == expert, logits, 0.0), axis=-1, keepdims=True)
    gates_ref[:, 0:1] = jax.nn.sigmoid(first - second)
    gates_ref[:, 1:2] = jax.nn.sigmoid(second - first)


def route(me, tokens, norm_gain, router_weight, ids, rows, slots, chunks):
    token_count, width = tokens.shape
    expert_count = router_weight.shape[1]
    vmem = pl.BlockSpec(memory_space=pltpu.VMEM)
    out = pl.pallas_call(
        functools.partial(route_kernel, rows, slots, expert_count, chunks),
        out_shape=tuple(jax.ShapeDtypeStruct((c, width), BF16) for c in chunks)
        + (jax.ShapeDtypeStruct((token_count, 2), F32),),
        in_specs=[pl.BlockSpec(memory_space=pltpu.SMEM), pl.BlockSpec(memory_space=pl.ANY)]
        + [vmem] * 4,
        out_specs=(vmem,) * (len(chunks) + 1),
        scratch_shapes=[pltpu.VMEM(tokens.shape, tokens.dtype), pltpu.SemaphoreType.DMA],
        compiler_params=pltpu.CompilerParams(vmem_limit_bytes=VMEM_LIMIT),
        name="route",
    )(me, tokens, norm_gain.reshape(1, width), router_weight.T, ids, ids.T)
    return out[:-1], out[-1]


def staged(fetches, ahead):
    def arrive(n):
        for c in fetches[n]:
            c.wait()
        if n + ahead < len(fetches):
            for c in fetches[n + ahead]:
                c.start()

    for c in [c for group in fetches[:ahead] for c in group]:
        c.start()
    return arrive


def up_kernel(block_count, *refs):
    blocks, refs = refs[:block_count], refs[block_count:]
    gate_ref, up_ref, hidden_ref, rows_ref, held_ref, sems, held_sems = refs
    buffers, _, _, tile = held_ref.shape
    copies, start, column = [], 0, 0
    for i, block in enumerate(blocks):
        size, part = block.shape
        target = rows_ref.at[pl.ds(start, size), pl.ds(column, part)]
        copies.append(pltpu.make_async_copy(block, target, sems.at[i]))
        column += part
        if column == rows_ref.shape[1]:
            start, column = start + size, 0
    for c in copies:
        c.start()
    fetches = []
    for j in range(gate_ref.shape[1] // tile):
        part, slot = pl.ds(j * tile, tile), j % buffers
        fetches.append(
            [
                pltpu.make_async_copy(r.at[:, part], held_ref.at[slot, i], held_sems.at[slot, i])
                for i, r in enumerate((gate_ref, up_ref))
            ]
        )
    arrive = staged(fetches, 2)
    for c in copies:
        c.wait()
    for j in range(len(fetches)):
        arrive(j)
        gate = jnp.dot(rows_ref[...], held_ref[j % buffers, 0], preferred_element_type=F32)
        up = jnp.dot(rows_ref[...], held_ref[j % buffers, 1], preferred_element_type=F32)
        hidden = gate / (1.0 + jnp.exp(-gate)) * up
        hidden_ref[:, j * tile : (j + 1) * tile] = hidden.astype(BF16)


def up_projection(blocks, gate_matrix, up_matrix):
    width, units = gate_matrix.shape
    rows = sum(b.size for b in blocks) // width
    buffers, tile = 3, 256
    return pl.pallas_call(
        functools.partial(up_kernel, len(blocks)),
        out_shape=jax.ShapeDtypeStruct((rows, units), BF16),
        in_specs=[pl.BlockSpec(memory_space=pl.ANY)] * (len(blocks) + 2),
        out_specs=pl.BlockSpec(memory_space=pltpu.VMEM),
        scratch_shapes=[
            pltpu.VMEM((rows, width), BF16),
            pltpu.VMEM((buffers, 2, width, tile), BF16),
            pltpu.SemaphoreType.DMA((len(blocks),)),
            pltpu.SemaphoreType.DMA((buffers, 2)),
        ],
        cost_estimate=pl.CostEstimate(
            flops=4 * rows * width * units,
            bytes_accessed=4 * width * units + 2 * rows * width,
            transcendentals=rows * units,
        ),
        compiler_params=pltpu.CompilerParams(vmem_limit_bytes=EXPERT_VMEM),
        name="up",
    )(*blocks, gate_matrix, up_matrix)


def down_kernel(out_count, hidden_ref, down_ref, *refs):
    out_refs, refs = refs[:out_count], refs[out_count:]
    held_ref, kept_ref, sent_ref, held_sems, out_sems = refs
    buffers, _, tile = held_ref.shape
    size, half = hidden_ref.shape[0] // out_count, out_count // 2
    fetches, stores = [], []
    for j in range(down_ref.shape[1] // tile):
        part, slot = pl.ds(j * tile, tile), j % buffers
        fetches.append(
            [pltpu.make_async_copy(down_ref.at[:, part], held_ref.at[slot], held_sems.at[slot])]
        )
        slot = j % kept_ref.shape[0]
        stores.append(
            [
                pltpu.make_async_copy(
                    (kept_ref if i < half else sent_ref).at[slot, pl.ds(i % half * size, size)],
                    out_ref.at[:, part],
                    out_sems.at[slot, i],
                )
                for i, out_ref in enumerate(out_refs)
            ]
        )
    arrive = staged(fetches, 2)
    slots = kept_ref.shape[0]
    for j in range(len(fetches)):
        arrive(j)
        out = jnp.dot(hidden_ref[...], held_ref[j % buffers], preferred_element_type=F32)
        if j >= slots:
            for c in stores[j - slots]:
                c.wait()
        kept_ref[j % slots] = out[: half * size]
        sent_ref[j % slots] = out[half * size :].astype(BF16)
        for c in stores[j]:
            c.start()
    for group in stores[-slots:]:
        for c in group:
            c.wait()


def down_projection(hidden, count, down_matrix):
    rows, (units, width) = hidden.shape[0], down_matrix.shape
    buffers, slots, tile = 3, 2, width // 4
    out = pl.pallas_call(
        functools.partial(down_kernel, count),
        out_shape=tuple(
            pltpu.HBM((rows // count, width), F32 if i < count // 2 else BF16)
            for i in range(count)
        ),
        in_specs=[pl.BlockSpec(memory_space=pltpu.VMEM), pl.BlockSpec(memory_space=pl.ANY)],
        out_specs=(pl.BlockSpec(memory_space=pltpu.HBM),) * count,
        scratch_shapes=[
            pltpu.VMEM((buffers, units, tile), BF16),
            pltpu.VMEM((slots, rows // 2, tile), F32),
            pltpu.VMEM((slots, rows // 2, tile), BF16),
            pltpu.SemaphoreType.DMA((buffers,)),
            pltpu.SemaphoreType.DMA((slots, count)),
        ],
        cost_estimate=pl.CostEstimate(
            flops=2 * rows * width * units,
            bytes_accessed=2 * width * units + 3 * rows * width,
            transcendentals=0,
        ),
        compiler_params=pltpu.CompilerParams(vmem_limit_bytes=DOWN_VMEM),
        name="down",
    )(hidden, down_matrix)
    return out[: count // 2], out[count // 2 :]


def combine_kernel(rows, slots, count, chunks, *refs):
    me, own_ref, ids_ref, gates_ref = refs[:4]
    taken_refs, out_ref = refs[4:-1], refs[-1]
    token_count = own_ref.shape[0]
    later = lax.broadcasted_iota(jnp.int32, (token_count, token_count), 0)
    earlier = lax.broadcasted_iota(jnp.int32, (token_count, token_count), 1)
    same = lax.div(earlier, rows) == lax.div(later, rows)
    before = jnp.where((earlier < later) & same, 1.0, 0.0).astype(BF16)
    token = lax.broadcasted_iota(jnp.int32, (token_count, 1), 0)
    expert = me[0] ^ lax.broadcasted_iota(jnp.int32, (token_count, 128), 1)
    named = (ids_ref[:, 0:1] == expert) | (ids_ref[:, 1:2] == expert)
    positions = jnp.dot(
        before, jnp.where(named, 1.0, 0.0).astype(BF16), preferred_element_type=F32
    ).astype(jnp.int32)
    total = own_ref[...].astype(F32)
    for k in range(count):
        which = me[0] ^ k
        first, second = ids_ref[:, 0:1] == which, ids_ref[:, 1:2] == which
        chosen = first | second
        slot = lax.div(token, rows) * slots + positions[:, k : k + 1]
        weight = jnp.where(first, gates_ref[:, 0:1], 0.0) + jnp.where(
            second, gates_ref[:, 1:2], 0.0
        )
        start, placed = 0, None
        for c, size in enumerate(chunks):
            held = lax.broadcasted_iota(jnp.int32, (token_count, size), 1) + start
            pick = jnp.where((held == slot) & chosen, 1.0, 0.0).astype(BF16)
            part = jnp.dot(pick, taken_refs[c * count + k][...], preferred_element_type=F32)
            placed = part if placed is None else placed + part
            start += size
        total += weight * placed
    out_ref[...] = total.astype(BF16)


def combine(me, own, ids, gates, taken, rows, slots, chunks):
    count = len(taken) // len(chunks)
    vmem = pl.BlockSpec(memory_space=pltpu.VMEM)
    return pl.pallas_call(
        functools.partial(combine_kernel, rows, slots, count, chunks),
        out_shape=jax.ShapeDtypeStruct(own.shape, BF16),
        in_specs=[pl.BlockSpec(memory_space=pltpu.SMEM)] + [vmem] * (3 + len(taken)),
        out_specs=vmem,
        compiler_params=pltpu.CompilerParams(vmem_limit_bytes=VMEM_LIMIT),
        name="combine",
    )(me, own, ids, gates, *taken)


def together(*groups):
    flat = lax.optimization_barrier([a for g in groups for a in g])
    return [[flat.pop(0) for _ in g] for g in groups]


def after(array, *earlier):
    return lax.optimization_barrier((array, *earlier))[0]


class Chunk:
    def __init__(self, own, bits):
        self.own, self.bits = own, bits

    def spread(self):
        self.held = {0: [self.own]}
        if len(self.bits) == 2:
            for bit in self.bits:
                self.held[bit] = [exchange(self.own, "dp", bit)]
        else:
            for bit in self.bits:
                for k, v in list(self.held.items()):
                    self.held[k | bit] = [exchange(p, "dp", bit) for p in v]

    def forward(self):
        if len(self.bits) == 2:
            a, b = self.bits
            half = self.own.shape[1] // 2
            left, right = self.held[b][0][:, :half], self.held[a][0][:, half:]
            self.held[a | b] = [exchange(left, "dp", a), exchange(right, "dp", b)]

    def up(self, matrices, *earlier):
        self.order = sorted(self.held)
        blocks = [p for k in self.order for p in self.held[k]]
        blocks = blocks + [exchange(block, "dp", 1) for block in blocks]
        if earlier:
            blocks[0] = after(blocks[0], *earlier)
        self.hidden = up_projection(blocks, *matrices[:2])

    def down(self, matrices):
        self.kept, self.sent = down_projection(self.hidden, 2 * len(self.order), matrices[2])

    def pair_sum(self):
        partner = [exchange(sent, "dp", 1) for sent in self.sent]
        width = self.own.shape[1]
        self.lanes = []
        for lane, bits in enumerate((self.bits, self.bits[::-1])):
            columns = slice(lane * width // 2, (lane + 1) * width // 2)
            terms = {
                k: [kept[:, columns], other[:, columns]]
                for k, kept, other in zip(self.order, self.kept, partner)
            }
            self.lanes.append((terms, bits))

    def leave(self, step):
        self.outgoing = []
        for terms, bits in self.lanes:
            leaving = sorted(k for k in terms if k & bits[step])
            self.outgoing.append(
                jnp.stack([sum(t.astype(F32) for t in terms[k]).astype(BF16) for k in leaving])
            )
        return self.outgoing

    def send(self, step):
        self.incoming = [
            exchange(out, "dp", bits[step]) for out, (_, bits) in zip(self.outgoing, self.lanes)
        ]

    def arrive(self, step):
        for incoming, (terms, bits) in zip(self.incoming, self.lanes):
            for i, k in enumerate(sorted(k for k in terms if k & bits[step])):
                terms[k ^ bits[step]] = terms[k ^ bits[step]] + [incoming[i]]
                del terms[k]

    def finish(self):
        sums = [sum(t.astype(F32) for t in terms[0]) for terms, _ in self.lanes]
        total = jnp.concatenate(sums, axis=1).astype(BF16)
        count, segment = lax.axis_size("segment"), lax.axis_index("segment")
        width = total.shape[1] // count
        parts = [
            lax.dynamic_slice_in_dim(total, (segment ^ k) * width, width, 1) for k in range(count)
        ]
        return [parts[0]] + [exchange(parts[k], "segment", k) for k in range(1, count)]


def per_device(tokens, norm_gain, router_weight, expert_ids, w_gate, w_up, w_down):
    micro_count, rows, width = tokens.shape
    expert_count = router_weight.shape[1]
    slots = 2 * rows // expert_count + rows // 8
    segment_count = lax.axis_size("segment")
    segment = lax.axis_index("segment")
    me = segment.astype(jnp.int32).reshape(1)
    bits = []
    while 2 ** (len(bits) + 1) < lax.axis_size("dp"):
        bits.append(2 ** (len(bits) + 1))
    slice_width = width // segment_count
    sizes = chunk_rows(micro_count * slots)
    flat = tokens.reshape(-1, width)
    ids = expert_ids.reshape(-1, 2)
    own_part = lax.dynamic_slice_in_dim(flat, segment * slice_width, slice_width, 1)
    routed, gates = route(me, flat, norm_gain, router_weight, ids, rows, slots, sizes)
    matrices = w_gate[0], w_up[0], w_down[0]
    one, two = (Chunk(own, bits) for own in routed)
    one.spread()
    two.own = after(two.own, *(p for b in bits for p in one.held[b]))
    two.spread()
    one.forward()
    one.up(matrices)
    hops = [b for b in sorted(two.held) if b]
    (one.hidden,), *arrived = together([one.hidden], *(two.held[b] for b in hops))
    two.held.update(zip(hops, arrived))
    two.forward()
    one.down(matrices)
    last = max(two.held)
    one.kept, one.sent, two.held[last] = together(one.kept, one.sent, two.held[last])
    one.pair_sum()
    steps = len(bits)
    one.leave(0)
    one.send(0)
    two.up(matrices, *one.outgoing)
    (two.hidden,), one.incoming = together([two.hidden], one.incoming)
    one.arrive(0)
    for step in range(1, steps):
        one.leave(step)
        one.send(step)
        if step < steps - 1:
            one.arrive(step)
    two.down(matrices)
    two.kept, two.sent, one.incoming = together(two.kept, two.sent, one.incoming)
    one.arrive(steps - 1)
    two.pair_sum()
    two.leave(0)
    two.send(0)
    taken = one.finish()
    for step in range(steps):
        if step < 1:
            share = slice(1, 3)
            taken[share], two.incoming = together(taken[share], two.incoming)
        two.arrive(step)
        if step + 1 < steps:
            two.leave(step + 1)
            two.send(step + 1)
    taken = taken + two.finish()
    out = combine(me, own_part, ids, gates, taken, rows, slots, sizes)
    return out.reshape(micro_count, rows, slice_width)


def solution(mesh):
    placed = (
        P(None, "dp", None),
        P(),
        P(),
        P(None, "dp", None),
        P("segment", None, "dp"),
        P("segment", None, "dp"),
        P("segment", "dp", None),
    )
    return jax.shard_map(
        per_device, mesh=mesh, in_specs=placed, out_specs=P(None, "dp", "segment"), check_vma=False
    )
```
